128 devices in a mesh: seq: 8 (over x_lo, z), fsdp: 16 (over y, x_hi, core).
Axes of the slice: x: 4 (x_hi: 2, x_lo: 2; x = x_hi * 2 + x_lo), y: 4, z: 4, core: 2. Of those that a mesh axis runs over, the one named last changes fastest.
Arguments:
- tokens: bfloat16 [32, 1024, 1024], P('fsdp', 'seq'), may hold values from -6 to 6
- cotangent: bfloat16 [32, 1024, 1024], P('fsdp', 'seq'), may hold values from -6 to 6
- attn_gain: bfloat16 [1024], P('fsdp'), may hold values from 0.5 to 1.5
- attn_shift: bfloat16 [1024], P('fsdp'), may hold values from -1.75 to 1.75
- mlp_gain: bfloat16 [1024], P('fsdp'), may hold values from 0.5 to 1.5
- mlp_shift: bfloat16 [1024], P('fsdp'), may hold values from -1.75 to 1.75
- qkv_weight: bfloat16 [1024, 3072], P('fsdp'), may hold values from -0.1875 to 0.1875
- qkv_bias: bfloat16 [3072], P('fsdp'), may hold values from -1.75 to 1.75
- out_weight: bfloat16 [1024, 1024], P('fsdp'), may hold values from -1.5 to 1.5
- out_bias: bfloat16 [1024], P('fsdp'), may hold values from -1.75 to 1.75
- up_weight: bfloat16 [1024, 4096], P('fsdp'), may hold values from -0.1875 to 0.1875
- up_bias: bfloat16 [4096], P('fsdp'), may hold values from -1.75 to 1.75
- down_weight: bfloat16 [4096, 1024], P('fsdp'), may hold values from -0.09375 to 0.09375
- down_bias: bfloat16 [1024], P('fsdp'), may hold values from -1.75 to 1.75
Outputs:
- out: bfloat16 [32, 1024, 1024], P('fsdp', 'seq')
- grad_input: bfloat16 [32, 1024, 1024], P('fsdp', 'seq')
- grad_attn_gain: float32 [1024], P('fsdp')
- grad_attn_shift: float32 [1024], P('fsdp')
- grad_mlp_gain: float32 [1024], P('fsdp')
- grad_mlp_shift: float32 [1024], P('fsdp')
- grad_qkv_weight: float32 [1024, 3072], P('fsdp')
- grad_qkv_bias: float32 [3072], P('fsdp')
- grad_out_weight: float32 [1024, 1024], P('fsdp')
- grad_out_bias: float32 [1024], P('fsdp')
- grad_up_weight: float32 [1024, 4096], P('fsdp')
- grad_up_bias: float32 [4096], P('fsdp')
- grad_down_weight: float32 [4096, 1024], P('fsdp')
- grad_down_bias: float32 [1024], P('fsdp')
The draws below stay inside these ranges and needn't reach their ends.
All inputs are finite; a program needn't handle non-finite values.
Results may differ from the reference program's by a relative error of at most 0.019.
Values may be sent and summed in bfloat16 or wider, within the bound.
No kernel may reach another device: no remote copies, remote signals or barrier semaphores. Data moves between devices by JAX's collectives and lax.ppermute only.
A program may use at most 192 MiB of HBM per device.

```python
import math
import jax
import jax.numpy as jnp
from jax import lax

D = 1024
HEADS = 16
HEAD_DIM = 64
ROTARY = 16
FF = 4096
LEN = 1024
SEQS = 32


def block_scale(key, dims, split, low, largest):
    level = 1.0
    for dim, parts in split:
        steps = jax.random.uniform(jax.random.fold_in(jax.random.fold_in(key, 6), dim), (parts,), jnp.float32, low / len(split), largest / len(split))
        level = level * jnp.repeat(jnp.exp(steps), dims[dim] // parts).reshape((-1,) + (1,) * (len(dims) - 1 - dim))
    return level


def normal_values(stream_key, dims, scale, bound, shards=(), kind=jnp.bfloat16):
    values = jax.random.normal(stream_key, dims, jnp.float32) * scale
    if len(shards) > 0:
        values = block_scale(stream_key, dims, shards, -0.22, 0.18) * values
    return jnp.clip(values, min=-bound, max=bound).astype(kind)


def setup_inputs(seed: int = 0) -> dict:
    arg_keys = jax.random.split(jax.random.key(seed), 15)
    tokens = normal_values(arg_keys[0], (SEQS, LEN, D), 1.0, 6.0, ((0, 16), (1, 8)))
    cotangent = normal_values(arg_keys[1], (SEQS, LEN, D), 1.0, 6.0, ((0, 16), (1, 8)))
    attn_gain = jnp.clip(1.0 + 0.1 * jax.random.normal(arg_keys[2], (D,), jnp.float32), 0.5, 1.5).astype(jnp.bfloat16)
    attn_shift = normal_values(arg_keys[3], (D,), 0.3, 1.75, ((0, 16),))
    mlp_gain = jnp.clip(1.0 + 0.1 * jax.random.normal(arg_keys[4], (D,), jnp.float32), 0.5, 1.5).astype(jnp.bfloat16)
    mlp_shift = normal_values(arg_keys[5], (D,), 0.3, 1.75, ((0, 16),))
    qkv_weight = normal_values(arg_keys[6], (D, 3 * D), D ** -0.5, 0.1875, ((0, 16),))
    qkv_bias = normal_values(arg_keys[7], (3 * D,), 0.3, 1.75, ((0, 16),))
    out_weight = normal_values(arg_keys[8], (D, D), (D // 64) ** -0.5, 1.5, ((0, 16),))
    out_bias = normal_values(arg_keys[9], (D,), 0.3, 1.75, ((0, 16),))
    up_weight = normal_values(arg_keys[10], (D, FF), D ** -0.5, 0.1875, ((0, 16),))
    up_bias = normal_values(arg_keys[11], (FF,), 0.3, 1.75, ((0, 16),))
    down_weight = normal_values(arg_keys[12], (FF, D), FF ** -0.5, 0.09375, ((0, 16),))
    down_bias = normal_values(arg_keys[13], (D,), 0.3, 1.75, ((0, 16),))
    return {"tokens": tokens, "cotangent": cotangent, "attn_gain": attn_gain, "attn_shift": attn_shift, "mlp_gain": mlp_gain, "mlp_shift": mlp_shift, "qkv_weight": qkv_weight, "qkv_bias": qkv_bias, "out_weight": out_weight, "out_bias": out_bias, "up_weight": up_weight, "up_bias": up_bias, "down_weight": down_weight, "down_bias": down_bias}


@jax.custom_vjp
def low(v):
    return lax.optimization_barrier(v.astype(jnp.bfloat16)).astype(jnp.float32)

@jax.custom_vjp
def low_back(v):
    return v

def low_keep(v):
    return (low(v), None)

def low_pass(kept, grad):
    return (grad,)

def back_keep(v):
    return (v, None)

def back_low(kept, grad):
    return (low(grad),)
low.defvjp(low_keep, low_pass)
low_back.defvjp(back_keep, back_low)

def both_ways(value):
    return low_back(low(value))

def layer_norm(rows, gain, shift):
    center = rows - lax.optimization_barrier(jnp.mean(rows, -1, keepdims=True))
    spread = lax.optimization_barrier(jnp.mean(center * center, -1, keepdims=True))
    return center * lax.rsqrt(spread + 1e-05) * gain + shift

def rotate(blocks, cosine, sine):
    half = ROTARY // 2
    first = blocks[..., :half]
    second = blocks[..., half:ROTARY]
    rest = blocks[..., ROTARY:]
    cos_b = cosine[:, None, :]
    sin_b = sine[:, None, :]
    return jnp.concatenate([first * cos_b - second * sin_b, second * cos_b + first * sin_b, rest], -1)

def rotary_tables():
    half = ROTARY // 2
    freq = 10000.0 ** (-(jnp.arange(half, dtype=jnp.float32) * 2.0 / ROTARY))
    angle = jnp.arange(LEN, dtype=jnp.float32)[:, None] * freq[None, :]
    return (jnp.cos(angle), jnp.sin(angle))

def attend_block(query_block, keyset, valueset, start):
    block = query_block.shape[0]
    stop = keyset.shape[0]
    scores = jnp.einsum('qhd,khd->hqk', query_block, keyset, precision=lax.Precision.HIGHEST) * HEAD_DIM ** (-0.5)
    scores = low_back(scores)
    allowed = jnp.arange(stop)[None, :] <= (start + jnp.arange(block))[:, None]
    scores = jnp.where(allowed[None], scores, -1e+30)
    top = lax.optimization_barrier(jnp.max(scores, -1, keepdims=True))
    expd = jnp.exp(scores - top)
    probs = low(expd / lax.optimization_barrier(jnp.sum(expd, -1, keepdims=True)))
    return jnp.einsum('hqk,khd->qhd', probs, valueset, precision=lax.Precision.HIGHEST)

def attend_sequence(queries, keyset, valueset):
    block = min(512, LEN)
    pieces = []
    for number in range(LEN // block):
        start = number * block
        stop = start + block
        func = jax.checkpoint(lambda qb, kb, vb, first=start: attend_block(qb, kb, vb, first))
        pieces.append(func(queries[start:stop], keyset[:stop], valueset[:stop]))
    return jnp.concatenate(pieces, 0)

def matmul(left, right):
    return jnp.einsum('gtd,de->gte', left, right, precision=lax.Precision.HIGHEST)

def layer(inputs, attn_gain, attn_shift, mlp_gain, mlp_shift, qkv_weight, qkv_bias, out_weight, out_bias, up_weight, up_bias, down_weight, down_bias):
    groups = inputs.shape[0]
    attn_in = low(layer_norm(inputs, attn_gain, attn_shift))
    mlp_in = low(layer_norm(inputs, mlp_gain, mlp_shift))
    projected = low_back(matmul(attn_in, qkv_weight) + qkv_bias)
    shape = (groups, LEN, HEADS, HEAD_DIM)
    cosine, sine = rotary_tables()
    queries = both_ways(rotate(projected[..., :D].reshape(shape), cosine, sine))
    keyset = both_ways(rotate(projected[..., D:2 * D].reshape(shape), cosine, sine))
    valueset = both_ways(projected[..., 2 * D:].reshape(shape))
    heads_out = jax.vmap(attend_sequence)(queries, keyset, valueset).reshape(groups, LEN, D)
    heads_out = both_ways(heads_out)
    attn_out = matmul(heads_out, out_weight) + out_bias
    hidden = low_back(matmul(mlp_in, up_weight) + up_bias)
    activated = low(jax.nn.gelu(hidden, approximate=False))
    mlp_out = matmul(activated, down_weight) + down_bias
    return inputs + attn_out + mlp_out

def reference(tokens, cotangent, attn_gain, attn_shift, mlp_gain, mlp_shift, qkv_weight, qkv_bias, out_weight, out_bias, up_weight, up_bias, down_weight, down_bias):
    params = (attn_gain, attn_shift, mlp_gain, mlp_shift, qkv_weight, qkv_bias, out_weight, out_bias, up_weight, up_bias, down_weight, down_bias)
    params = jax.tree.map(lambda leaf: leaf.astype(jnp.float32), params)
    groups = math.gcd(SEQS, max(1, 4096 // LEN))
    count = SEQS // groups
    inputs_all = tokens.astype(jnp.float32).reshape(count, groups, LEN, D)
    grads_all = cotangent.astype(jnp.float32).reshape(count, groups, LEN, D)

    def scan_step(total, pair):
        inputs, grads_in = pair
        result, pull = jax.vjp(layer, inputs, *params)
        back = pull(grads_in)
        total = jax.tree.map(jnp.add, total, tuple(back[1:]))
        return (total, (result, back[0]))
    init = jax.tree.map(jnp.zeros_like, params)
    total, (outputs, grad_in) = lax.scan(scan_step, init, (inputs_all, grads_all))
    out = outputs.reshape(SEQS, LEN, D).astype(jnp.bfloat16)
    grad_input = grad_in.reshape(SEQS, LEN, D).astype(jnp.bfloat16)
    return (out, grad_input, total[0], total[1], total[2], total[3], total[4], total[5], total[6], total[7], total[8], total[9], total[10], total[11])
```

```python
import functools

import jax
import jax.numpy as jnp
import numpy as np
from jax import lax
from jax.experimental import pallas as pl
from jax.experimental.pallas import tpu as pltpu
from jax.sharding import Mesh
from jax.sharding import PartitionSpec as P

HEAD_DIM = 64
ROTARY = 16
LEN = 1024
ROWS = 1024
BLOCK = 256
SEQ = ("xl", "z")
FSDP = ("y", "xh", "c")
F32 = jnp.float32
LOW = jnp.bfloat16
SCALE = HEAD_DIM ** (-0.5)


def dot(left, right, dims):
    return lax.dot_general(left, right, (dims, ((), ())), preferred_element_type=F32)


def plain(left, right):
    return dot(left, right, ((1,), (0,)))


def spread(block, axes, count):
    return lax.all_to_all(jnp.broadcast_to(block[None], (count,) + block.shape), axes, 0, 0)


def flip(block, axis, bit=1):
    size = 4 if axis in ("z", "y") else 2
    return lax.ppermute(block, axis, [(a, a ^ bit) for a in range(size)])


def across(block):
    return lax.ppermute(block, ("xl", "xh"), [(0, 3), (3, 0), (1, 2), (2, 1)])


def swap(block):
    return lax.ppermute(block, ("z", "y"), [(a * 4 + b, b * 4 + a) for a in range(4) for b in range(4)])


def rotary_tables():
    half = ROTARY // 2
    freq = np.float32(10000.0) ** (-(np.arange(half, dtype=np.float32) * np.float32(2.0 / ROTARY)))
    angle = np.arange(LEN, dtype=np.float32)[:, None] * freq[None, :]
    cosine = np.ones((LEN, HEAD_DIM), np.float32)
    sine = np.zeros((LEN, HEAD_DIM), np.float32)
    cosine[:, :half] = cosine[:, half:ROTARY] = np.cos(angle)
    sine[:, :half] = -np.sin(angle)
    sine[:, half:ROTARY] = np.sin(angle)
    return np.tile(cosine, (1, 2)), np.tile(sine, (1, 2))


def partner(rows):
    lane = lax.broadcasted_iota(jnp.int32, rows.shape, 1) % HEAD_DIM
    return jnp.where(lane < ROTARY // 2, pltpu.roll(rows, 120, 1), pltpu.roll(rows, 8, 1))


def head_lanes(rows, head):
    lane = lax.broadcasted_iota(jnp.int32, rows.shape, 1) // HEAD_DIM
    return jnp.where(lane == head, rows, jnp.zeros_like(rows))


def place_qkv(index_ref, own, other, out_ref, rest_ref):
    c = index_ref[4]
    for spot, block in ((c, own), (1 - c, other)):
        out_ref[:, spot] = block[:, :64]
        rest_ref[:, spot] = block[:, 64:]


def place_mlp(index_ref, own, other, up_ref, rest_ref, down_ref):
    c = index_ref[4]
    for spot, block in ((c, own), (1 - c, other)):
        up_ref[:, spot] = block[:, :64]
        rest_ref[:, spot] = block[:, 64:80]
        lanes = pl.ds(pl.multiple_of(spot * 512, 512), 512)
        down_ref[:, :64, lanes] = block[:, 80:, :512]
        down_ref[:, 64:, lanes] = block[:, 80:, 512:]


def place_out(index_ref, own, over, core, both, out_ref):
    xh, c = index_ref[3], index_ref[4]
    out_ref[xh, c] = own[...]
    out_ref[1 - xh, c] = over[...]
    out_ref[xh, 1 - c] = core[...]
    out_ref[1 - xh, 1 - c] = both[...]


def added(one, two):
    return (one.astype(F32) + two.astype(F32)).astype(LOW)


def pack_mlp(index_ref, cols, cols_got, rows, rows_got, out_own, out_over, out_got, lines, pack_ref):
    xl, c = index_ref[0], index_ref[4]
    up = added(cols[:, c], cols_got[...])
    down = added(rows[:, :, pl.ds(pl.multiple_of(c * 512, 512), 512)], rows_got[...])
    mine = added(out_own[c], out_got[0])
    over = added(out_over[c], out_got[1])
    first = jnp.where(xl == 0, mine, over)
    last = jnp.where(xl == 0, over, mine)
    for half in range(2):
        lanes = slice(half * 512, (half + 1) * 512)
        pack_ref[:, half, :, :64] = up[:, :, lanes].reshape(4, 2, 64, 512)
        pack_ref[:, half, :, 80:144] = down[:, half * 64 : (half + 1) * 64].reshape(4, 2, 64, 512)
        for y in range(4):
            for xh, block in enumerate((first, last)):
                pack_ref[y, half, xh, 64:80] = lines[half]
                pack_ref[y, half, xh, 144:] = block[y * 16 : y * 16 + 16, lanes]


def pack_qkv(index_ref, own, own_got, over, over_got, lines, pack_ref):
    xl, c = index_ref[0], index_ref[4]
    for half, block, got in ((xl, own, own_got), (1 - xl, over, over_got)):
        dest = pl.ds(pl.multiple_of(half * 8, 8), 8)
        pack_ref[dest, :64] = added(block[:, c], got[...])
    for spot in range(16):
        pack_ref[spot, 64:] = lines[spot // 8]


def finish(
    index_ref, sums, qkv, up, gains, grad_qkv, grad_up, grad_out, bias, qkv_sums, up_sums, rows_ref
):
    def lanes(start):
        return slice(start, start + 128)

    scale = [jnp.broadcast_to(gains[:, i : i + 1], (64, 128)) for i in range(4)]
    totals = [jnp.zeros((64, 128), F32) for i in range(4)]
    for xl in range(2):
        bias[:, xl * 512 : xl * 512 + 512] = sums[xl, 0, 64:80].astype(F32)[1:2]
        for z in range(4):
            grad_out[z * 16 : z * 16 + 16, xl * 512 : xl * 512 + 512] = sums[xl, z, 144:160].astype(F32)
            for part in range(4):
                block = sums[xl, z, :64, lanes(part * 128)].astype(F32)
                line = sums[xl, z, 64:80, lanes(part * 128)].astype(F32)[0:1]
                spot = lanes(((xl * 4 + part) * 4 + z) * 128)
                weight = up[:, spot].astype(F32)
                totals[2] += weight * block
                totals[3] += weight * line
                grad_up[:, spot] = scale[2] * block + scale[3] * line
                up_sums[:, spot] = line
            for part in range(3):
                block = sums[xl, z, 160:224, lanes(part * 128)].astype(F32)
                line = sums[xl, z, 224:240, lanes(part * 128)].astype(F32)[0:1]
                spot = lanes(part * 1024 + z * 256 + xl * 128)
                weight = qkv[:, spot].astype(F32)
                totals[0] += weight * block
                totals[1] += weight * line
                grad_qkv[:, spot] = scale[0] * block + scale[1] * line
                qkv_sums[:, spot] = line
    rows_ref[...] = jnp.concatenate([jnp.sum(total, 1, keepdims=True) for total in totals], 1)


def finish_down(index_ref, sums, got, out_ref):
    c = index_ref[4]
    for spot in range(4):
        xl, z = spot % 2, spot // 2
        rows = slice(spot * 64, spot * 64 + 64)
        own = sums[xl, c * 2 + z, 80:144].astype(F32)
        out_ref[rows, pl.ds(pl.multiple_of(c * 512, 512), 512)] = own
        out_ref[rows, pl.ds(pl.multiple_of((1 - c) * 512, 512), 512)] = got[xl, z].astype(F32)


def place(kernel, name, index, blocks, shapes, kind=LOW):
    def whole(shape):
        return pl.BlockSpec(shape, lambda i, index: (0,) * len(shape))

    return pl.pallas_call(
        kernel,
        grid_spec=pltpu.PrefetchScalarGridSpec(
            num_scalar_prefetch=1,
            grid=(1,),
            in_specs=[whole(block.shape) for block in blocks],
            out_specs=[whole(shape) for shape in shapes],
        ),
        out_shape=[jax.ShapeDtypeStruct(shape, kind) for shape in shapes],
        compiler_params=PARAMS,
        name=name,
    )(index, *blocks)


def load(index_ref, own_ref, other_refs, part):
    xl = index_ref[0]
    lanes = slice(part * 128, (part + 1) * 128)
    each = 4 // len(other_refs)
    blocks = []
    for number in range(8):
        spot = number % 4
        other = other_refs[spot // each][spot % each, 0, :, lanes]
        blocks.append(jnp.where(xl == number // 4, own_ref[spot, 0, :, lanes], other))
    return jnp.concatenate(blocks, 0)


def store(index_ref, done_ref, own_ref, other_refs):
    xl = index_ref[0]
    each = 4 // len(other_refs)
    for number in range(4):
        own_ref[number, 0] = done_ref[xl * 4 + number]
        other_refs[number // each][number % each, 0] = done_ref[(1 - xl) * 4 + number]


def rotated(index_ref, own_ref, other_ref, cos_ref, sin_ref):
    q = load(index_ref, own_ref, other_ref, 0).astype(F32)
    k = load(index_ref, own_ref, other_ref, 1).astype(F32)
    cosine, sine = cos_ref[...], sin_ref[...]
    q = ((q * cosine + partner(q) * sine) * SCALE).astype(LOW)
    k = (k * cosine + partner(k) * sine).astype(LOW)
    return q, k


def diagonal():
    keys = lax.broadcasted_iota(jnp.int32, (BLOCK, BLOCK), 0)
    return keys <= lax.broadcasted_iota(jnp.int32, (BLOCK, BLOCK), 1)


def forward_kernel(index_ref, x_ref, y0_ref, y1_ref, cos_ref, sin_ref, own_ref, other_ref, total_ref, done_ref):
    y_ref = (y0_ref, y1_ref)
    q, k = rotated(index_ref, x_ref, y_ref, cos_ref, sin_ref)
    vt = load(index_ref, x_ref, y_ref, 2).T
    allowed = diagonal()
    for number in range(LEN // BLOCK):
        start, stop = number * BLOCK, (number + 1) * BLOCK
        outs = []
        for head in range(2):
            qb = head_lanes(q[start:stop], head)
            last = dot(k[start:stop], qb, ((1,), (1,)))
            last = jnp.where(allowed, last, -1e30)
            top = jnp.max(last, 0, keepdims=True)
            if start:
                first = dot(k[:start], qb, ((1,), (1,)))
                top = jnp.maximum(top, jnp.max(first, 0, keepdims=True))
            last = jnp.exp(last - top)
            total = jnp.sum(last, 0, keepdims=True)
            rows = vt[head * HEAD_DIM : (head + 1) * HEAD_DIM]
            out = plain(rows[:, start:stop], last.astype(LOW))
            if start:
                first = jnp.exp(first - top)
                total = total + jnp.sum(first, 0, keepdims=True)
                out = out + plain(rows[:, :start], first.astype(LOW))
            outs.append(out / total)
            total_ref[0, head : head + 1, start:stop] = top + jnp.log(total)
        out = jnp.concatenate(outs, 0).T.astype(LOW)
        done_ref[2 * number : 2 * number + 2] = out.reshape(2, 128, 128)
    store(index_ref, done_ref, own_ref, (other_ref,))


def backward_kernel(
    index_ref,
    x_ref,
    y0_ref,
    y1_ref,
    g_ref,
    h_ref,
    total_ref,
    cos_ref,
    sin_ref,
    own_ref,
    over0_ref,
    over1_ref,
    dk_ref,
    dv_ref,
    done_ref,
):
    y_ref = (y0_ref, y1_ref)
    q, k = rotated(index_ref, x_ref, y_ref, cos_ref, sin_ref)
    v = load(index_ref, x_ref, y_ref, 2)
    kt = k.T
    g = load(index_ref, g_ref, (h_ref,), 0)
    allowed = diagonal()
    for number in range(LEN // BLOCK):
        start, stop = number * BLOCK, (number + 1) * BLOCK
        outs = []
        for head in range(2):
            qb = head_lanes(q[start:stop], head)
            gb = head_lanes(g[start:stop], head)
            total = total_ref[0, head : head + 1, start:stop]
            p1 = jnp.exp(dot(k[start:stop], qb, ((1,), (1,))) - total)
            p1 = jnp.where(allowed, p1, 0.0)
            d1 = dot(v[start:stop], gb, ((1,), (1,)))
            delta = jnp.sum(p1 * d1, 0, keepdims=True)
            if start:
                p0 = jnp.exp(dot(k[:start], qb, ((1,), (1,))) - total)
                d0 = dot(v[:start], gb, ((1,), (1,)))
                delta = delta + jnp.sum(p0 * d0, 0, keepdims=True)
            d1 = (p1 * (d1 - delta)).astype(LOW)
            rows = kt[head * HEAD_DIM : (head + 1) * HEAD_DIM]
            out = plain(rows[:, start:stop], d1)
            dv1 = plain(p1.astype(LOW), gb)
            dk1 = plain(d1, qb)
            if head == 0:
                dv_ref[start:stop] = dv1
                dk_ref[start:stop] = dk1
            else:
                dv_ref[start:stop] += dv1
                dk_ref[start:stop] += dk1
            if start:
                d0 = (p0 * (d0 - delta)).astype(LOW)
                out = out + plain(rows[:, :start], d0)
                dv_ref[:start] += plain(p0.astype(LOW), gb)
                dk_ref[:start] += plain(d0, qb)
            outs.append(out)
        dq = jnp.concatenate(outs, 0).T * SCALE
        dq = dq * cos_ref[start:stop] - partner(dq) * sin_ref[start:stop]
        done_ref[2 * number : 2 * number + 2, :, :128] = dq.astype(LOW).reshape(2, 128, 128)
    dk = dk_ref[...]
    dk = dk * cos_ref[...] - partner(dk) * sin_ref[...]
    done_ref[:, :, 128:256] = dk.astype(LOW).reshape(8, 128, 128)
    done_ref[:, :, 256:] = dv_ref[...].astype(LOW).reshape(8, 128, 128)
    store(index_ref, done_ref, own_ref, (over0_ref, over1_ref))


def half_spec(width, count=4):
    return pl.BlockSpec((count, 1, 128, width), lambda s, index: (0, s, 0, 0))


def half_shape(width, count=4):
    return jax.ShapeDtypeStruct((count, 2, 128, width), LOW)


TABLE = pl.BlockSpec((LEN, 128), lambda s, index: (0, 0))
STATS = pl.BlockSpec((1, 2, LEN), lambda s, index: (s, 0, 0))
PARAMS = pltpu.CompilerParams(vmem_limit_bytes=32 * 1024 * 1024)
ATTEND = pltpu.CompilerParams(vmem_limit_bytes=60 * 1024 * 1024)


def attend_forward(index, x, y0, y1, cosine, sine):
    return pl.pallas_call(
        forward_kernel,
        grid_spec=pltpu.PrefetchScalarGridSpec(
            num_scalar_prefetch=1,
            grid=(2,),
            in_specs=[half_spec(384), half_spec(384, 2), half_spec(384, 2), TABLE, TABLE],
            out_specs=[half_spec(128), half_spec(128), STATS],
            scratch_shapes=[pltpu.VMEM((8, 128, 128), LOW)],
        ),
        out_shape=[half_shape(128), half_shape(128), jax.ShapeDtypeStruct((2, 2, LEN), F32)],
        compiler_params=ATTEND,
        cost_estimate=pl.CostEstimate(flops=4 * 10**9, bytes_accessed=4 * 2**20, transcendentals=2 * 2**20),
        name="attend_forward",
    )(index, x, y0, y1, cosine, sine)


def attend_backward(index, x, y0, y1, g, h, total, cosine, sine):
    return pl.pallas_call(
        backward_kernel,
        grid_spec=pltpu.PrefetchScalarGridSpec(
            num_scalar_prefetch=1,
            grid=(2,),
            in_specs=[
                half_spec(384),
                half_spec(384, 2),
                half_spec(384, 2),
                half_spec(128),
                half_spec(128),
                STATS,
                TABLE,
                TABLE,
            ],
            out_specs=[half_spec(384), half_spec(384, 2), half_spec(384, 2)],
            scratch_shapes=[
                pltpu.VMEM((LEN, 128), F32),
                pltpu.VMEM((LEN, 128), F32),
                pltpu.VMEM((8, 128, 384), LOW),
            ],
        ),
        out_shape=[half_shape(384), half_shape(384, 2), half_shape(384, 2)],
        compiler_params=ATTEND,
        cost_estimate=pl.CostEstimate(flops=8 * 10**9, bytes_accessed=6 * 2**20, transcendentals=2 * 2**20),
        name="attend_backward",
    )(index, x, y0, y1, g, h, total, cosine, sine)


def shards(
    tokens,
    cotangent,
    attn_gain,
    attn_shift,
    mlp_gain,
    mlp_shift,
    qkv_weight,
    qkv_bias,
    out_weight,
    out_bias,
    up_weight,
    up_bias,
    down_weight,
    down_bias,
):
    xl, z, y, xh, c = (lax.axis_index(name) for name in SEQ + FSDP)
    index = jnp.stack([xl, z, y, xh, c]).astype(jnp.int32)
    owner = y * 4 + xh * 2 + c
    gain_one = attn_gain.astype(F32)[:, None]
    gain_two = mlp_gain.astype(F32)[:, None]
    shift_one = attn_shift.astype(F32)[:, None]
    shift_two = mlp_shift.astype(F32)[:, None]

    def pick(values, number, axis):
        return lax.dynamic_index_in_dim(values, number, axis, keepdims=False)

    def cut(values, number, size, axis):
        return lax.dynamic_slice_in_dim(values, number * size, size, axis)

    def of_z(values):
        lead = values.shape[0]
        return pick(values.reshape(lead, 3, 4, 2, 128), z, 2).transpose(0, 2, 1, 3).reshape(lead, 768)

    def units_of_z(values):
        lead = values.shape[0]
        return pick(values.reshape(lead, 8, 4, 128), z, 2).reshape(lead, 1024)

    def placed(part, size):
        return lax.dynamic_update_slice(jnp.zeros((size,), F32), part.astype(F32), (owner * part.shape[0],))

    def two_parts(values):
        high = lax.reduce_precision(values, 8, 7)
        return [high.astype(LOW)[None], (values - high).astype(LOW)[None]]

    def block_of(weight, gain, shift, bias, more):
        wide = weight.astype(F32)
        lines = two_parts(jnp.sum(wide * shift, 0) + bias)
        for values in more:
            lines = lines + two_parts(values)
        lines.append(jnp.zeros((16 - len(lines), weight.shape[1]), LOW))
        return jnp.concatenate([(wide * gain).astype(LOW)] + lines, 0)

    def with_neighbour(own):
        over = across(own)
        return jnp.where(xh == 0, jnp.stack([own, over]), jnp.stack([over, own]))

    def over_owners(pair):
        return spread(pair, "y", 4).reshape((8,) + pair.shape[1:])

    def whole_lines(lines):
        lines = jnp.sum(lines.astype(F32), (0, 1))
        return lines[0::2] + lines[1::2]

    rows = tokens.reshape(256, 1024).astype(F32)
    center = rows - jnp.mean(rows, -1, keepdims=True)
    inverse = lax.rsqrt(jnp.mean(center * center, -1, keepdims=True) + 1e-05)
    norm = center * inverse
    norm_all = lax.all_gather(norm.astype(LOW), "z", axis=0, tiled=True)
    grad_low = cotangent.reshape(256, 1024)
    grad_all = lax.all_gather(grad_low, "z", axis=0, tiled=True)

    block = block_of(of_z(qkv_weight), gain_one, shift_one, of_z(placed(qkv_bias, 3072)[None])[0], [])
    out_block = swap(out_weight)
    down_block = cut(down_weight, z % 2, 128, 0)
    down_block = jnp.where(
        c == z // 2, cut(down_block, c, 512, 1), flip(cut(down_block, 1 - c, 512, 1), "c")
    )
    down_block = jnp.concatenate([down_block[:64], down_block[64:]], 1)
    mlp_block = block_of(
        units_of_z(up_weight),
        gain_two,
        shift_two,
        units_of_z(placed(up_bias, 4096)[None])[0],
        [placed(out_bias, 1024) + placed(down_bias, 1024)],
    )
    mlp_block = jnp.concatenate([mlp_block, down_block], 0)
    block, mlp_block, out_block = lax.optimization_barrier(
        (with_neighbour(block), with_neighbour(mlp_block), out_block)
    )
    block = over_owners(block)
    out_over = across(out_block)
    (out_full,) = place(
        place_out,
        "place_out",
        index,
        (out_block, out_over, flip(out_block, "c"), flip(out_over, "c")),
        [(2, 2, 64, 1024)],
    )
    out_full = out_full.reshape(256, 1024)

    qkv_full, lines = place(
        place_qkv, "place_qkv", index, (block, flip(block, "c")), [(8, 2, 64, 768), (8, 2, 16, 768)]
    )
    qkv_full = qkv_full.reshape(1024, 768)
    qkv_add = whole_lines(lines)[0]

    mlp_block, block = lax.optimization_barrier((mlp_block, block))
    mlp_block = over_owners(mlp_block)

    def sum_over_z(part):
        return lax.psum_scatter(part, "z", scatter_dimension=0, tiled=True)

    def project(values, number):
        weight = cut(qkv_full, number, 384, 1)
        return (plain(values, weight) + cut(qkv_add, number, 384, 0)).astype(LOW).reshape(-1, 2, 128, 384)

    qkv_over = [flip(project(norm_all[half * 512 : half * 512 + 512], 1 - xl), "xl") for half in range(2)]
    qkv_own = project(norm_all, xl)
    qkv_over[0], out_full = lax.optimization_barrier((qkv_over[0], out_full))
    cosine, sine = rotary_tables()
    done_own, done_over, totals = attend_forward(index, qkv_own, *qkv_over, cosine, sine)
    mlp_block, totals = lax.optimization_barrier((mlp_block, totals))
    up_full, lines, down_full = place(
        place_mlp,
        "place_mlp",
        index,
        (mlp_block, flip(mlp_block, "c")),
        [(8, 2, 64, 1024), (8, 2, 16, 1024), (8, 128, 1024)],
    )
    up_full = up_full.reshape(1024, 1024)
    down_full = down_full.reshape(1024, 1024)
    lines = whole_lines(lines)
    up_add, out_add = lines[0], lines[1]

    hidden = plain(norm_all, up_full) + up_add
    below = 0.5 * (1.0 + lax.erf(hidden * np.float32(0.5**0.5)))
    density = jnp.exp(-0.5 * hidden * hidden) * np.float32(1.0 / np.sqrt(2.0 * np.pi))
    active, slope = lax.optimization_barrier(
        ((hidden * below).astype(LOW), (below + hidden * density).astype(LOW))
    )
    done_own, done_over, grad_heads = lax.optimization_barrier((done_own, done_over, grad_all))
    done_over = flip(done_over, "xl").reshape(ROWS, 128)
    def head_grads(number):
        return dot(grad_heads, cut(out_full, number, 128, 0), ((1,), (1,))).astype(LOW)

    heads_over = flip(head_grads(1 - xl), "xl").reshape(4, 2, 128, 128)
    heads_own = head_grads(xl).reshape(4, 2, 128, 128)
    done_own = done_own.reshape(ROWS, 128)
    out_mine, out_other = cut(out_full, xl, 128, 0), cut(out_full, 1 - xl, 128, 0)
    grad_hidden = (dot(grad_all, down_full, ((1,), (1,))) * slope.astype(F32)).astype(LOW)
    def across_tokens(left, right):
        return dot(left, right, ((0,), (0,))).astype(LOW)

    grad_rows = across_tokens(active, grad_all).reshape(8, 128, 1024)
    grad_cols = across_tokens(norm_all, grad_hidden).reshape(8, 2, 64, 1024)
    outs_own = across_tokens(done_own, grad_all).reshape(2, 64, 1024)
    outs_over = across_tokens(done_over, grad_all).reshape(2, 64, 1024)
    outs_sent = jnp.stack([pick(outs_own, 1 - c, 0), pick(outs_over, 1 - c, 0)])
    rows_got = flip(cut(grad_rows, 1 - c, 512, 2), "c")
    cols_got = flip(pick(grad_cols, 1 - c, 1), "c")
    outs_got = flip(outs_sent, "c")

    def lines_of(values, width):
        values = (values + flip(values, "c")).astype(LOW).reshape(-1, 2, width).transpose(1, 0, 2)
        return jnp.concatenate([values, jnp.zeros((2, 16 - values.shape[1], width), LOW)], 1)

    def summed(blocks):
        return jnp.sum(lax.all_to_all(blocks, ("xl", "y", "xh"), 0, 0).astype(F32), 0).astype(LOW)

    sums = jnp.concatenate(
        [jnp.sum(grad_hidden.astype(F32), 0)[None], jnp.sum(grad_all.astype(F32), 0)[None]], 0
    )
    (pack,) = place(
        pack_mlp,
        "pack_mlp",
        index,
        (grad_cols, cols_got, grad_rows, rows_got, outs_own, outs_over, outs_got, lines_of(sums, 512)),
        [(4, 2, 2, 160, 512)],
    )
    pack, heads_own = lax.optimization_barrier((pack, heads_own))
    mlp_sum = lax.all_to_all(pack, "y", 0, 0)
    mlp_sum = jnp.sum(mlp_sum.astype(F32), 0).astype(LOW).reshape(4, 160, 512)
    gq_own, *gq_over = attend_backward(index, qkv_own, *qkv_over, heads_own, heads_over, totals, cosine, sine)
    gq_own, gq_over, active = lax.optimization_barrier((gq_own, gq_over, active))
    gq_over = jnp.concatenate([flip(part, "xl") for part in gq_over], 0)
    result = plain(active, down_full) + plain(done_own, out_mine) + plain(done_over, out_other)
    result, mlp_sum, gq_own, gq_over = lax.optimization_barrier(
        (result.astype(LOW), mlp_sum, gq_own, gq_over)
    )
    result = sum_over_z(result)
    mlp_sum = lax.all_to_all(mlp_sum, ("xl", "xh"), 0, 0)
    gq_over = gq_over.reshape(ROWS, 384)
    gq_own = gq_own.reshape(ROWS, 384)

    qkv_part = across_tokens(norm_all, gq_own).reshape(8, 2, 64, 384)
    qkv_over_part = across_tokens(norm_all, gq_over).reshape(8, 2, 64, 384)
    sums = jnp.stack([jnp.sum(gq_own.astype(F32), 0), jnp.sum(gq_over.astype(F32), 0)])
    sums = jnp.where(xl == 0, sums, sums[::-1]).reshape(1, 768)
    (pack,) = place(
        pack_qkv,
        "pack_qkv",
        index,
        (
            qkv_part,
            flip(pick(qkv_part, 1 - c, 1), "c"),
            qkv_over_part,
            flip(pick(qkv_over_part, 1 - c, 1), "c"),
            lines_of(sums, 384),
        ),
        [(16, 80, 384)],
    )
    pack, mlp_sum, gq_own, gq_over = lax.optimization_barrier((pack, mlp_sum, gq_own, gq_over))
    attn_sum = summed(pack)

    qkv_mine, qkv_other = cut(qkv_full, xl, 384, 1), cut(qkv_full, 1 - xl, 384, 1)
    incoming = (
        dot(grad_hidden, up_full, ((1,), (1,)))
        + dot(gq_own, qkv_mine, ((1,), (1,)))
        + dot(gq_over, qkv_other, ((1,), (1,)))
    )
    incoming, result = lax.optimization_barrier((incoming.astype(LOW), result))
    incoming = sum_over_z(incoming).astype(F32)
    result = (rows + result.astype(F32) + out_add).astype(LOW).reshape(tokens.shape)
    grad_input = grad_low.astype(F32) + inverse * (
        incoming
        - jnp.mean(incoming, -1, keepdims=True)
        - norm * jnp.mean(incoming * norm, -1, keepdims=True)
    )
    grad_input = grad_input.astype(LOW).reshape(tokens.shape)

    mlp_sum = jnp.sum(mlp_sum.astype(F32), 0).astype(LOW)
    mlp_sum = jnp.concatenate([mlp_sum[:144], swap(mlp_sum[144:])], 0)
    sums = jnp.concatenate([mlp_sum, jnp.pad(attn_sum, ((0, 0), (0, 128)))], 0)
    sums = spread(sums, SEQ, 8).reshape(2, 4, 240, 512)
    sums, grad_input, result = lax.optimization_barrier((sums, grad_input, result))
    gains = jnp.concatenate([gain_one, shift_one, gain_two, shift_two], 1)
    grad_qkv, grad_up, grad_out, grad_bias, qkv_total, up_total, grad_rows = place(
        finish,
        "finish",
        index,
        (sums, qkv_weight, up_weight, gains),
        [(64, 3072), (64, 4096), (64, 1024), (1, 1024), (1, 3072), (1, 4096), (64, 4)],
        F32,
    )
    down_over = flip(pick(sums.reshape(2, 2, 2, 240, 512), 1 - c, 1)[:, :, 80:144], "c")
    (grad_down,) = place(finish_down, "finish_down", index, (sums, down_over), [(256, 1024)], F32)
    grad_bias = cut(grad_bias[0], owner, 64, 0)
    return (
        result,
        grad_input,
        grad_rows[:, 0],
        grad_rows[:, 1],
        grad_rows[:, 2],
        grad_rows[:, 3],
        grad_qkv,
        cut(qkv_total[0], owner, 192, 0),
        grad_out,
        grad_bias,
        grad_up,
        cut(up_total[0], owner, 256, 0),
        grad_down,
        grad_bias,
    )


def solution(mesh):
    fine = Mesh(mesh.devices.reshape(2, 4, 4, 2, 2), SEQ + FSDP)
    row = P(FSDP, SEQ, None)
    flat, tall = P(FSDP), P(FSDP, None)
    specs = (flat, flat, flat, flat, tall, flat, tall, flat, tall, flat, tall, flat)
    return jax.shard_map(
        shards, mesh=fine, in_specs=(row, row) + specs, out_specs=(row, row) + specs, check_vma=False
    )
```

```python
import functools

import jax
import jax.numpy as jnp
import numpy as np
from jax import lax
from jax.experimental import pallas as pl
from jax.experimental.pallas import tpu as pltpu
from jax.sharding import Mesh
from jax.sharding import PartitionSpec as P

HEAD_DIM = 64
ROTARY = 16
LEN = 1024
ROWS = 1024
BLOCK = 256
SEQ = ("xl", "z")
FSDP = ("y", "xh", "c")
F32 = jnp.float32
LOW = jnp.bfloat16
SCALE = HEAD_DIM ** (-0.5)


def dot(left, right, dims):
    return lax.dot_general(left, right, (dims, ((), ())), preferred_element_type=F32)


def plain(left, right):
    return dot(left, right, ((1,), (0,)))


def spread(block, axes, count):
    return lax.all_to_all(jnp.broadcast_to(block[None], (count,) + block.shape), axes, 0, 0)


def flip(block, axis, bit=1):
    size = 4 if axis in ("z", "y") else 2
    return lax.ppermute(block, axis, [(a, a ^ bit) for a in range(size)])


def across(block):
    return lax.ppermute(block, ("xl", "xh"), [(0, 3), (3, 0), (1, 2), (2, 1)])


def swap(block):
    return lax.ppermute(block, ("z", "y"), [(a * 4 + b, b * 4 + a) for a in range(4) for b in range(4)])


def rotary_tables():
    half = ROTARY // 2
    freq = np.float32(10000.0) ** (-(np.arange(half, dtype=np.float32) * np.float32(2.0 / ROTARY)))
    angle = np.arange(LEN, dtype=np.float32)[:, None] * freq[None, :]
    cosine = np.ones((LEN, HEAD_DIM), np.float32)
    sine = np.zeros((LEN, HEAD_DIM), np.float32)
    cosine[:, :half] = cosine[:, half:ROTARY] = np.cos(angle)
    sine[:, :half] = -np.sin(angle)
    sine[:, half:ROTARY] = np.sin(angle)
    return np.tile(cosine, (1, 2)), np.tile(sine, (1, 2))


def partner(rows):
    lane = lax.broadcasted_iota(jnp.int32, rows.shape, 1) % HEAD_DIM
    return jnp.where(lane < ROTARY // 2, pltpu.roll(rows, 120, 1), pltpu.roll(rows, 8, 1))


def head_lanes(rows, head):
    lane = lax.broadcasted_iota(jnp.int32, rows.shape, 1) // HEAD_DIM
    return jnp.where(lane == head, rows, jnp.zeros_like(rows))


def place_qkv(index_ref, own, other, out_ref, rest_ref):
    c = index_ref[4]
    for spot, block in ((c, own), (1 - c, other)):
        out_ref[:, spot] = block[:, :64]
        rest_ref[:, spot] = block[:, 64:]


def place_mlp(index_ref, own, other, up_ref, rest_ref, down_ref):
    c = index_ref[4]
    for spot, block in ((c, own), (1 - c, other)):
        up_ref[:, spot] = block[:, :64]
        rest_ref[:, spot] = block[:, 64:80]
        lanes = pl.ds(pl.multiple_of(spot * 512, 512), 512)
        down_ref[:, :64, lanes] = block[:, 80:, :512]
        down_ref[:, 64:, lanes] = block[:, 80:, 512:]


def place_out(index_ref, own, over, core, both, out_ref):
    xh, c = index_ref[3], index_ref[4]
    out_ref[xh, c] = own[...]
    out_ref[1 - xh, c] = over[...]
    out_ref[xh, 1 - c] = core[...]
    out_ref[1 - xh, 1 - c] = both[...]


def added(one, two):
    return (one.astype(F32) + two.astype(F32)).astype(LOW)


def pack_mlp(index_ref, cols, cols_got, rows, rows_got, out_own, out_over, out_got, lines, pack_ref):
    xl, c = index_ref[0], index_ref[4]
    up = added(cols[:, c], cols_got[...])
    down = added(rows[:, :, pl.ds(pl.multiple_of(c * 512, 512), 512)], rows_got[...])
    mine = added(out_own[c], out_got[0])
    over = added(out_over[c], out_got[1])
    first = jnp.where(xl == 0, mine, over)
    last = jnp.where(xl == 0, over, mine)
    for half in range(2):
        lanes = slice(half * 512, (half + 1) * 512)
        pack_ref[:, half, :, :64] = up[:, :, lanes].reshape(4, 2, 64, 512)
        pack_ref[:, half, :, 80:144] = down[:, half * 64 : (half + 1) * 64].reshape(4, 2, 64, 512)
        for y in range(4):
            for xh, block in enumerate((first, last)):
                pack_ref[y, half, xh, 64:80] = lines[half]
                pack_ref[y, half, xh, 144:] = block[y * 16 : y * 16 + 16, lanes]


def pack_qkv(index_ref, own, own_got, over, over_got, lines, pack_ref):
    xl, c = index_ref[0], index_ref[4]
    for half, block, got in ((xl, own, own_got), (1 - xl, over, over_got)):
        dest = pl.ds(pl.multiple_of(half * 8, 8), 8)
        pack_ref[dest, :64] = added(block[:, c], got[...])
    for spot in range(16):
        pack_ref[spot, 64:] = lines[spot // 8]


def finish(
    index_ref, sums, qkv, up, gains, grad_qkv, grad_up, grad_out, bias, qkv_sums, up_sums, rows_ref
):
    def lanes(start):
        return slice(start, start + 128)

    scale = [jnp.broadcast_to(gains[:, i : i + 1], (64, 128)) for i in range(4)]
    totals = [jnp.zeros((64, 128), F32) for i in range(4)]
    for xl in range(2):
        bias[:, xl * 512 : xl * 512 + 512] = sums[xl, 0, 64:80].astype(F32)[1:2]
        for z in range(4):
            grad_out[z * 16 : z * 16 + 16, xl * 512 : xl * 512 + 512] = sums[xl, z, 144:160].astype(F32)
            for part in range(4):
                block = sums[xl, z, :64, lanes(part * 128)].astype(F32)
                line = sums[xl, z, 64:80, lanes(part * 128)].astype(F32)[0:1]
                spot = lanes(((xl * 4 + part) * 4 + z) * 128)
                weight = up[:, spot].astype(F32)
                totals[2] += weight * block
                totals[3] += weight * line
                grad_up[:, spot] = scale[2] * block + scale[3] * line
                up_sums[:, spot] = line
            for part in range(3):
                tail = 160 + part * 16
                block = jnp.concatenate(
                    [sums[xl, z, 160:208, lanes(part * 128)], sums[xl, z, tail : tail + 16, lanes(384)]], 0
                ).astype(F32)
                line = sums[xl, z, 64:80, lanes(part * 128)].astype(F32)[2:3]
                spot = lanes(part * 1024 + z * 256 + xl * 128)
                weight = qkv[:, spot].astype(F32)
                totals[0] += weight * block
                totals[1] += weight * line
                grad_qkv[:, spot] = scale[0] * block + scale[1] * line
                qkv_sums[:, spot] = line
    rows_ref[...] = jnp.concatenate([jnp.sum(total, 1, keepdims=True) for total in totals], 1)


def finish_down(index_ref, sums, got, out_ref):
    c = index_ref[4]
    for spot in range(4):
        xl, z = spot % 2, spot // 2
        rows = slice(spot * 64, spot * 64 + 64)
        own = sums[xl, c * 2 + z, 80:144].astype(F32)
        out_ref[rows, pl.ds(pl.multiple_of(c * 512, 512), 512)] = own
        out_ref[rows, pl.ds(pl.multiple_of((1 - c) * 512, 512), 512)] = got[xl, z].astype(F32)


def place(kernel, name, index, blocks, shapes, kind=LOW):
    def whole(shape):
        return pl.BlockSpec(shape, lambda i, index: (0,) * len(shape))

    return pl.pallas_call(
        kernel,
        grid_spec=pltpu.PrefetchScalarGridSpec(
            num_scalar_prefetch=1,
            grid=(1,),
            in_specs=[whole(block.shape) for block in blocks],
            out_specs=[whole(shape) for shape in shapes],
        ),
        out_shape=[jax.ShapeDtypeStruct(shape, kind) for shape in shapes],
        compiler_params=PARAMS,
        name=name,
    )(index, *blocks)


def load(index_ref, own_ref, other_refs, part):
    xl = index_ref[0]
    lanes = slice(part * 128, (part + 1) * 128)
    each = 4 // len(other_refs)
    blocks = []
    for number in range(8):
        spot = number % 4
        other = other_refs[spot // each][spot % each, 0, :, lanes]
        blocks.append(jnp.where(xl == number // 4, own_ref[spot, 0, :, lanes], other))
    return jnp.concatenate(blocks, 0)


def store(index_ref, done_ref, own_ref, other_refs):
    xl = index_ref[0]
    each = 4 // len(other_refs)
    for number in range(4):
        own_ref[number, 0] = done_ref[xl * 4 + number]
        other_refs[number // each][number % each, 0] = done_ref[(1 - xl) * 4 + number]


def rotated(index_ref, own_ref, other_ref, cos_ref, sin_ref):
    q = load(index_ref, own_ref, other_ref, 0).astype(F32)
    k = load(index_ref, own_ref, other_ref, 1).astype(F32)
    cosine, sine = cos_ref[...], sin_ref[...]
    q = ((q * cosine + partner(q) * sine) * SCALE).astype(LOW)
    k = (k * cosine + partner(k) * sine).astype(LOW)
    return q, k


def diagonal():
    keys = lax.broadcasted_iota(jnp.int32, (BLOCK, BLOCK), 0)
    return keys <= lax.broadcasted_iota(jnp.int32, (BLOCK, BLOCK), 1)


def forward_kernel(index_ref, x_ref, y0_ref, y1_ref, cos_ref, sin_ref, own_ref, other_ref, total_ref, done_ref):
    y_ref = (y0_ref, y1_ref)
    q, k = rotated(index_ref, x_ref, y_ref, cos_ref, sin_ref)
    vt = load(index_ref, x_ref, y_ref, 2).T
    allowed = diagonal()
    for number in range(LEN // BLOCK):
        start, stop = number * BLOCK, (number + 1) * BLOCK
        outs = []
        for head in range(2):
            qb = head_lanes(q[start:stop], head)
            last = dot(k[start:stop], qb, ((1,), (1,)))
            last = jnp.where(allowed, last, -1e30)
            top = jnp.max(last, 0, keepdims=True)
            if start:
                first = dot(k[:start], qb, ((1,), (1,)))
                top = jnp.maximum(top, jnp.max(first, 0, keepdims=True))
            last = jnp.exp(last - top)
            total = jnp.sum(last, 0, keepdims=True)
            rows = vt[head * HEAD_DIM : (head + 1) * HEAD_DIM]
            out = plain(rows[:, start:stop], last.astype(LOW))
            if start:
                first = jnp.exp(first - top)
                total = total + jnp.sum(first, 0, keepdims=True)
                out = out + plain(rows[:, :start], first.astype(LOW))
            outs.append(out / total)
            total_ref[0, head : head + 1, start:stop] = top + jnp.log(total)
        out = jnp.concatenate(outs, 0).T.astype(LOW)
        done_ref[2 * number : 2 * number + 2] = out.reshape(2, 128, 128)
    store(index_ref, done_ref, own_ref, (other_ref,))


def backward_kernel(
    index_ref,
    x_ref,
    y0_ref,
    y1_ref,
    g_ref,
    h_ref,
    total_ref,
    cos_ref,
    sin_ref,
    own_ref,
    over0_ref,
    over1_ref,
    dk_ref,
    dv_ref,
    done_ref,
):
    y_ref = (y0_ref, y1_ref)
    q, k = rotated(index_ref, x_ref, y_ref, cos_ref, sin_ref)
    v = load(index_ref, x_ref, y_ref, 2)
    kt = k.T
    g = load(index_ref, g_ref, (h_ref,), 0)
    allowed = diagonal()
    for number in range(LEN // BLOCK):
        start, stop = number * BLOCK, (number + 1) * BLOCK
        outs = []
        for head in range(2):
            qb = head_lanes(q[start:stop], head)
            gb = head_lanes(g[start:stop], head)
            total = total_ref[0, head : head + 1, start:stop]
            p1 = jnp.exp(dot(k[start:stop], qb, ((1,), (1,))) - total)
            p1 = jnp.where(allowed, p1, 0.0)
            d1 = dot(v[start:stop], gb, ((1,), (1,)))
            delta = jnp.sum(p1 * d1, 0, keepdims=True)
            if start:
                p0 = jnp.exp(dot(k[:start], qb, ((1,), (1,))) - total)
                d0 = dot(v[:start], gb, ((1,), (1,)))
                delta = delta + jnp.sum(p0 * d0, 0, keepdims=True)
            d1 = (p1 * (d1 - delta)).astype(LOW)
            rows = kt[head * HEAD_DIM : (head + 1) * HEAD_DIM]
            out = plain(rows[:, start:stop], d1)
            dv1 = plain(p1.astype(LOW), gb)
            dk1 = plain(d1, qb)
            if head == 0:
                dv_ref[start:stop] = dv1
                dk_ref[start:stop] = dk1
            else:
                dv_ref[start:stop] += dv1
                dk_ref[start:stop] += dk1
            if start:
                d0 = (p0 * (d0 - delta)).astype(LOW)
                out = out + plain(rows[:, :start], d0)
                dv_ref[:start] += plain(p0.astype(LOW), gb)
                dk_ref[:start] += plain(d0, qb)
            outs.append(out)
        dq = jnp.concatenate(outs, 0).T * SCALE
        dq = dq * cos_ref[start:stop] - partner(dq) * sin_ref[start:stop]
        done_ref[2 * number : 2 * number + 2, :, :128] = dq.astype(LOW).reshape(2, 128, 128)
    dk = dk_ref[...]
    dk = dk * cos_ref[...] - partner(dk) * sin_ref[...]
    done_ref[:, :, 128:256] = dk.astype(LOW).reshape(8, 128, 128)
    done_ref[:, :, 256:] = dv_ref[...].astype(LOW).reshape(8, 128, 128)
    store(index_ref, done_ref, own_ref, (over0_ref, over1_ref))


def half_spec(width, count=4):
    return pl.BlockSpec((count, 1, 128, width), lambda s, index: (0, s, 0, 0))


def half_shape(width, count=4):
    return jax.ShapeDtypeStruct((count, 2, 128, width), LOW)


TABLE = pl.BlockSpec((LEN, 128), lambda s, index: (0, 0))
STATS = pl.BlockSpec((1, 2, LEN), lambda s, index: (s, 0, 0))
PARAMS = pltpu.CompilerParams(vmem_limit_bytes=32 * 1024 * 1024)
ATTEND = pltpu.CompilerParams(vmem_limit_bytes=60 * 1024 * 1024)


def attend_forward(index, x, y0, y1, cosine, sine):
    return pl.pallas_call(
        forward_kernel,
        grid_spec=pltpu.PrefetchScalarGridSpec(
            num_scalar_prefetch=1,
            grid=(2,),
            in_specs=[half_spec(384), half_spec(384, 2), half_spec(384, 2), TABLE, TABLE],
            out_specs=[half_spec(128), half_spec(128), STATS],
            scratch_shapes=[pltpu.VMEM((8, 128, 128), LOW)],
        ),
        out_shape=[half_shape(128), half_shape(128), jax.ShapeDtypeStruct((2, 2, LEN), F32)],
        compiler_params=ATTEND,
        cost_estimate=pl.CostEstimate(flops=4 * 10**9, bytes_accessed=4 * 2**20, transcendentals=2 * 2**20),
        name="attend_forward",
    )(index, x, y0, y1, cosine, sine)


def attend_backward(index, x, y0, y1, g, h, total, cosine, sine):
    return pl.pallas_call(
        backward_kernel,
        grid_spec=pltpu.PrefetchScalarGridSpec(
            num_scalar_prefetch=1,
            grid=(2,),
            in_specs=[
                half_spec(384),
                half_spec(384, 2),
                half_spec(384, 2),
                half_spec(128),
                half_spec(128),
                STATS,
                TABLE,
                TABLE,
            ],
            out_specs=[half_spec(384), half_spec(384, 2), half_spec(384, 2)],
            scratch_shapes=[
                pltpu.VMEM((LEN, 128), F32),
                pltpu.VMEM((LEN, 128), F32),
                pltpu.VMEM((8, 128, 384), LOW),
            ],
        ),
        out_shape=[half_shape(384), half_shape(384, 2), half_shape(384, 2)],
        compiler_params=ATTEND,
        cost_estimate=pl.CostEstimate(flops=8 * 10**9, bytes_accessed=6 * 2**20, transcendentals=2 * 2**20),
        name="attend_backward",
    )(index, x, y0, y1, g, h, total, cosine, sine)


def shards(
    tokens,
    cotangent,
    attn_gain,
    attn_shift,
    mlp_gain,
    mlp_shift,
    qkv_weight,
    qkv_bias,
    out_weight,
    out_bias,
    up_weight,
    up_bias,
    down_weight,
    down_bias,
):
    xl, z, y, xh, c = (lax.axis_index(name) for name in SEQ + FSDP)
    index = jnp.stack([xl, z, y, xh, c]).astype(jnp.int32)
    owner = y * 4 + xh * 2 + c
    gain_one = attn_gain.astype(F32)[:, None]
    gain_two = mlp_gain.astype(F32)[:, None]
    shift_one = attn_shift.astype(F32)[:, None]
    shift_two = mlp_shift.astype(F32)[:, None]

    def pick(values, number, axis):
        return lax.dynamic_index_in_dim(values, number, axis, keepdims=False)

    def cut(values, number, size, axis):
        return lax.dynamic_slice_in_dim(values, number * size, size, axis)

    def of_z(values):
        lead = values.shape[0]
        return pick(values.reshape(lead, 3, 4, 2, 128), z, 2).transpose(0, 2, 1, 3).reshape(lead, 768)

    def units_of_z(values):
        lead = values.shape[0]
        return pick(values.reshape(lead, 8, 4, 128), z, 2).reshape(lead, 1024)

    def placed(part, size):
        return lax.dynamic_update_slice(jnp.zeros((size,), F32), part.astype(F32), (owner * part.shape[0],))

    def two_parts(values):
        high = lax.reduce_precision(values, 8, 7)
        return [high.astype(LOW)[None], (values - high).astype(LOW)[None]]

    def block_of(weight, gain, shift, bias, more):
        wide = weight.astype(F32)
        lines = two_parts(jnp.sum(wide * shift, 0) + bias)
        for values in more:
            lines = lines + two_parts(values)
        lines.append(jnp.zeros((16 - len(lines), weight.shape[1]), LOW))
        return jnp.concatenate([(wide * gain).astype(LOW)] + lines, 0)

    def with_neighbour(own):
        over = across(own)
        return jnp.where(xh == 0, jnp.stack([own, over]), jnp.stack([over, own]))

    def over_owners(pair):
        return spread(pair, "y", 4).reshape((8,) + pair.shape[1:])

    def whole_lines(lines):
        lines = jnp.sum(lines.astype(F32), (0, 1))
        return lines[0::2] + lines[1::2]

    rows = tokens.reshape(256, 1024).astype(F32)
    center = rows - jnp.mean(rows, -1, keepdims=True)
    inverse = lax.rsqrt(jnp.mean(center * center, -1, keepdims=True) + 1e-05)
    norm = center * inverse
    norm_all = lax.all_gather(norm.astype(LOW), "z", axis=0, tiled=True)
    grad_low = cotangent.reshape(256, 1024)
    grad_all = lax.all_gather(grad_low, "z", axis=0, tiled=True)

    block = block_of(of_z(qkv_weight), gain_one, shift_one, of_z(placed(qkv_bias, 3072)[None])[0], [])
    out_block = swap(out_weight)
    down_block = cut(down_weight, z % 2, 128, 0)
    down_block = jnp.where(
        c == z // 2, cut(down_block, c, 512, 1), flip(cut(down_block, 1 - c, 512, 1), "c")
    )
    down_block = jnp.concatenate([down_block[:64], down_block[64:]], 1)
    mlp_block = block_of(
        units_of_z(up_weight),
        gain_two,
        shift_two,
        units_of_z(placed(up_bias, 4096)[None])[0],
        [placed(out_bias, 1024) + placed(down_bias, 1024)],
    )
    mlp_block = jnp.concatenate([mlp_block, down_block], 0)
    block, mlp_block, out_block = lax.optimization_barrier(
        (with_neighbour(block), with_neighbour(mlp_block), out_block)
    )
    block = over_owners(block)
    out_over = across(out_block)
    (out_full,) = place(
        place_out,
        "place_out",
        index,
        (out_block, out_over, flip(out_block, "c"), flip(out_over, "c")),
        [(2, 2, 64, 1024)],
    )
    out_full = out_full.reshape(256, 1024)

    qkv_full, lines = place(
        place_qkv, "place_qkv", index, (block, flip(block, "c")), [(8, 2, 64, 768), (8, 2, 16, 768)]
    )
    qkv_full = qkv_full.reshape(1024, 768)
    qkv_add = whole_lines(lines)[0]

    mlp_block, block = lax.optimization_barrier((mlp_block, block))
    mlp_block = over_owners(mlp_block)

    def sum_over_z(part):
        return lax.psum_scatter(part, "z", scatter_dimension=0, tiled=True)

    def project(values, number):
        weight = cut(qkv_full, number, 384, 1)
        return (plain(values, weight) + cut(qkv_add, number, 384, 0)).astype(LOW).reshape(-1, 2, 128, 384)

    qkv_over = [flip(project(norm_all[half * 512 : half * 512 + 512], 1 - xl), "xl") for half in range(2)]
    qkv_own = project(norm_all, xl)
    qkv_over[0], out_full = lax.optimization_barrier((qkv_over[0], out_full))
    cosine, sine = rotary_tables()
    done_own, done_over, totals = attend_forward(index, qkv_own, *qkv_over, cosine, sine)
    mlp_block, totals = lax.optimization_barrier((mlp_block, totals))
    up_full, lines, down_full = place(
        place_mlp,
        "place_mlp",
        index,
        (mlp_block, flip(mlp_block, "c")),
        [(8, 2, 64, 1024), (8, 2, 16, 1024), (8, 128, 1024)],
    )
    up_full = up_full.reshape(1024, 1024)
    down_full = down_full.reshape(1024, 1024)
    lines = whole_lines(lines)
    up_add, out_add = lines[0], lines[1]

    hidden = plain(norm_all, up_full) + up_add
    below = 0.5 * (1.0 + lax.erf(hidden * np.float32(0.5**0.5)))
    density = jnp.exp(-0.5 * hidden * hidden) * np.float32(1.0 / np.sqrt(2.0 * np.pi))
    active, slope = lax.optimization_barrier(
        ((hidden * below).astype(LOW), (below + hidden * density).astype(LOW))
    )
    done_own, done_over, grad_heads = lax.optimization_barrier((done_own, done_over, grad_all))
    done_over = flip(done_over, "xl").reshape(ROWS, 128)
    def head_grads(number):
        return dot(grad_heads, cut(out_full, number, 128, 0), ((1,), (1,))).astype(LOW)

    heads_over = flip(head_grads(1 - xl), "xl").reshape(4, 2, 128, 128)
    heads_own = head_grads(xl).reshape(4, 2, 128, 128)
    done_own = done_own.reshape(ROWS, 128)
    out_mine, out_other = cut(out_full, xl, 128, 0), cut(out_full, 1 - xl, 128, 0)
    grad_hidden = (dot(grad_all, down_full, ((1,), (1,))) * slope.astype(F32)).astype(LOW)
    def across_tokens(left, right):
        return dot(left, right, ((0,), (0,))).astype(LOW)

    grad_rows = across_tokens(active, grad_all).reshape(8, 128, 1024)
    grad_cols = across_tokens(norm_all, grad_hidden).reshape(8, 2, 64, 1024)
    outs_own = across_tokens(done_own, grad_all).reshape(2, 64, 1024)
    outs_over = across_tokens(done_over, grad_all).reshape(2, 64, 1024)
    outs_sent = jnp.stack([pick(outs_own, 1 - c, 0), pick(outs_over, 1 - c, 0)])
    rows_got = flip(cut(grad_rows, 1 - c, 512, 2), "c")
    cols_got = flip(pick(grad_cols, 1 - c, 1), "c")
    outs_got = flip(outs_sent, "c")

    def lines_of(values, width):
        values = (values + flip(values, "c")).astype(LOW).reshape(-1, 2, width).transpose(1, 0, 2)
        return jnp.concatenate([values, jnp.zeros((2, 16 - values.shape[1], width), LOW)], 1)

    def summed(blocks):
        return jnp.sum(lax.all_to_all(blocks, ("xl", "y", "xh"), 0, 0).astype(F32), 0).astype(LOW)

    sums = jnp.concatenate(
        [jnp.sum(grad_hidden.astype(F32), 0)[None], jnp.sum(grad_all.astype(F32), 0)[None]], 0
    )
    (pack,) = place(
        pack_mlp,
        "pack_mlp",
        index,
        (grad_cols, cols_got, grad_rows, rows_got, outs_own, outs_over, outs_got, lines_of(sums, 512)),
        [(4, 2, 2, 160, 512)],
    )
    pack, heads_own = lax.optimization_barrier((pack, heads_own))
    mlp_sum = lax.all_to_all(pack, "y", 0, 0)
    mlp_sum = jnp.sum(mlp_sum.astype(F32), 0).astype(LOW).reshape(4, 160, 512)
    gq_own, *gq_over = attend_backward(index, qkv_own, *qkv_over, heads_own, heads_over, totals, cosine, sine)
    gq_own, gq_over, active = lax.optimization_barrier((gq_own, gq_over, active))
    gq_over = jnp.concatenate([flip(part, "xl") for part in gq_over], 0)
    result = plain(active, down_full) + plain(done_own, out_mine) + plain(done_over, out_other)
    result, mlp_sum, gq_own, gq_over = lax.optimization_barrier(
        (result.astype(LOW), mlp_sum, gq_own, gq_over)
    )
    result = sum_over_z(result)
    mlp_sum = lax.all_to_all(mlp_sum, ("xl", "xh"), 0, 0)
    gq_over = gq_over.reshape(ROWS, 384)
    gq_own = gq_own.reshape(ROWS, 384)

    qkv_part = across_tokens(norm_all, gq_own).reshape(8, 2, 64, 384)
    qkv_over_part = across_tokens(norm_all, gq_over).reshape(8, 2, 64, 384)
    sums = jnp.stack([jnp.sum(gq_own.astype(F32), 0), jnp.sum(gq_over.astype(F32), 0)])
    sums = jnp.where(xl == 0, sums, sums[::-1]).reshape(1, 768)
    (pack,) = place(
        pack_qkv,
        "pack_qkv",
        index,
        (
            qkv_part,
            flip(pick(qkv_part, 1 - c, 1), "c"),
            qkv_over_part,
            flip(pick(qkv_over_part, 1 - c, 1), "c"),
            lines_of(sums, 384),
        ),
        [(16, 80, 384)],
    )
    pack, mlp_sum, gq_own, gq_over = lax.optimization_barrier((pack, mlp_sum, gq_own, gq_over))
    attn_sum = summed(pack)

    qkv_mine, qkv_other = cut(qkv_full, xl, 384, 1), cut(qkv_full, 1 - xl, 384, 1)
    incoming = (
        dot(grad_hidden, up_full, ((1,), (1,)))
        + dot(gq_own, qkv_mine, ((1,), (1,)))
        + dot(gq_over, qkv_other, ((1,), (1,)))
    )
    incoming, result = lax.optimization_barrier((incoming.astype(LOW), result))
    incoming = sum_over_z(incoming).astype(F32)
    result = (rows + result.astype(F32) + out_add).astype(LOW).reshape(tokens.shape)
    grad_input = grad_low.astype(F32) + inverse * (
        incoming
        - jnp.mean(incoming, -1, keepdims=True)
        - norm * jnp.mean(incoming * norm, -1, keepdims=True)
    )
    grad_input = grad_input.astype(LOW).reshape(tokens.shape)

    mlp_sum = jnp.sum(mlp_sum.astype(F32), 0).astype(LOW)
    mlp_sum = jnp.concatenate([mlp_sum[:144], swap(mlp_sum[144:])], 0)
    tail = jnp.concatenate([attn_sum[48:64, part * 128 : part * 128 + 128] for part in range(3)], 0)
    mlp_sum = lax.dynamic_update_slice(mlp_sum, attn_sum[64:65], (66, 0))
    sums = jnp.concatenate([mlp_sum, jnp.concatenate([attn_sum[:48], tail], 1)], 0)
    sums = spread(sums, SEQ, 8).reshape(2, 4, 208, 512)
    sums, grad_input, result = lax.optimization_barrier((sums, grad_input, result))
    gains = jnp.concatenate([gain_one, shift_one, gain_two, shift_two], 1)
    grad_qkv, grad_up, grad_out, grad_bias, qkv_total, up_total, grad_rows = place(
        finish,
        "finish",
        index,
        (sums, qkv_weight, up_weight, gains),
        [(64, 3072), (64, 4096), (64, 1024), (1, 1024), (1, 3072), (1, 4096), (64, 4)],
        F32,
    )
    down_over = flip(pick(sums.reshape(2, 2, 2, 208, 512), 1 - c, 1)[:, :, 80:144], "c")
    (grad_down,) = place(finish_down, "finish_down", index, (sums, down_over), [(256, 1024)], F32)
    grad_bias = cut(grad_bias[0], owner, 64, 0)
    return (
        result,
        grad_input,
        grad_rows[:, 0],
        grad_rows[:, 1],
        grad_rows[:, 2],
        grad_rows[:, 3],
        grad_qkv,
        cut(qkv_total[0], owner, 192, 0),
        grad_out,
        grad_bias,
        grad_up,
        cut(up_total[0], owner, 256, 0),
        grad_down,
        grad_bias,
    )


def solution(mesh):
    fine = Mesh(mesh.devices.reshape(2, 4, 4, 2, 2), SEQ + FSDP)
    row = P(FSDP, SEQ, None)
    flat, tall = P(FSDP), P(FSDP, None)
    specs = (flat, flat, flat, flat, tall, flat, tall, flat, tall, flat, tall, flat)
    return jax.shard_map(
        shards, mesh=fine, in_specs=(row, row) + specs, out_specs=(row, row) + specs, check_vma=False
    )
```
